32 devices in a mesh: patch: 8 (over z, x), feat: 4 (over y, core).
Axes of the slice: x: 2, y: 2, z: 4, core: 2. Of those that a mesh axis runs over, the one named last changes fastest.
Arguments:
- node_latents: bfloat16 [4096, 512], P('patch'), may hold values from -6 to 6
- edge_latents: bfloat16 [32768, 512], P('patch'), may hold values from -6 to 6
- send_rows: int32 [8, 8, 128], P('patch'), may hold values from 0 to 511, as said below
- edge_slot: int32 [32768], P('patch'), may hold values from 0 to 1023, as said below
- receivers: int32 [32768], P('patch'), may hold values from 0 to 511
- edge_in_w: bfloat16 [3, 3, 512, 512], P(None, None, None, 'feat'), may hold values from -0.15625 to 0.15625
- edge_in_b: float32 [3, 512], P(None, 'feat'), may hold values from -3 to 3
- edge_out_w: bfloat16 [3, 512, 512], P(None, 'feat'), may hold values from -0.25 to 0.25
- edge_gain: float32 [3, 512], replicated, may hold values from 0.5 to 2
- node_in_w: bfloat16 [3, 2, 512, 512], P(None, None, None, 'feat'), may hold values from -0.1875 to 0.1875
- node_in_b: float32 [3, 512], P(None, 'feat'), may hold values from -3 to 3
- node_out_w: bfloat16 [3, 512, 512], P(None, 'feat'), may hold values from -0.25 to 0.25
- node_gain: float32 [3, 512], replicated, may hold values from 0.5 to 2
Outputs:
- node_state: bfloat16 [4096, 512], P('patch')
- edge_state: bfloat16 [32768, 512], P('patch')
The draws below stay inside these ranges and needn't reach their ends.
Inputs may be any that keep to these rules, and one draw needn't show every extreme that they name: `send_rows`: the rows that one pair (s, d) names at slots used by some edge are distinct; unused slots hold 0. Every edge of patch d names a used slot of some patch s. Each patch names its last node row in the first slot it provides to itself. `edge_slot`: every patch holds exactly 4096 edges, all ending at its own nodes.
All inputs are finite; a program needn't handle non-finite values.
Results may differ from the reference program's by a relative error of at most 0.023.
Values may be sent and summed in bfloat16 or wider, within the bound.
A program may use at most 128 MiB of HBM per device.

```python
import math
import jax
import jax.numpy as jnp
from jax import lax

D = 512
H = 512
NODE_DEV = 512
LAYERS = 3
EDGE_DEV = 4096
CAP = 128
PEERS = 8
NODES = 4096
EDGES = 32768
N_FEAT = 4


def route_plan(key):
    count_key = jax.random.fold_in(key, 101)
    row_key = jax.random.fold_in(key, 102)
    edge_key = jax.random.fold_in(key, 103)
    source_idx = jnp.arange(PEERS, dtype=jnp.int32)[:, None]
    target_idx = jnp.arange(PEERS, dtype=jnp.int32)[None, :]
    apart_gap = jnp.abs(source_idx - target_idx)
    cycle_gap = jnp.minimum(apart_gap, PEERS - apart_gap)
    sparse_counts = jax.random.randint(count_key, (PEERS, PEERS), max(CAP // 8, 1), CAP // 2 + 1)
    counts = jnp.where(cycle_gap <= 2, CAP, sparse_counts)
    row_keys = jax.random.split(row_key, PEERS * PEERS)

    def pick_rows(subkey):
        return jax.random.permutation(subkey, NODE_DEV)[:CAP]
    chosen = jax.vmap(pick_rows)(row_keys).reshape(PEERS, PEERS, CAP).astype(jnp.int32)
    leading = chosen[:, :, 0:1]
    rotated = (chosen + (NODE_DEV - 1) - leading) % NODE_DEV
    on_diag = (source_idx == target_idx)[:, :, None]
    chosen = jnp.where(on_diag, rotated, chosen).astype(jnp.int32)
    in_use = jnp.arange(CAP, dtype=jnp.int32)[None, None, :] < counts[:, :, None]
    row_table = jnp.where(in_use, chosen, 0).astype(jnp.int32)
    return (in_use, row_table, edge_key)


def edges_for(used_flat, subkey):
    ordering = jnp.argsort(jnp.where(used_flat, 0, 1).astype(jnp.int32), stable=True).astype(jnp.int32)
    live_count = jnp.sum(used_flat.astype(jnp.int32))
    pick_key, shuffle_key = jax.random.split(subkey)
    extra_pick = jax.random.randint(pick_key, (EDGE_DEV,), 0, live_count)
    positions = jnp.arange(EDGE_DEV, dtype=jnp.int32)
    picked = jnp.where(positions < live_count, positions, extra_pick)
    slot_list = ordering[picked]
    return jax.random.permutation(shuffle_key, slot_list)


def draw_send_rows(key, part):
    in_use, row_table, edge_key = route_plan(key)
    return row_table


def draw_edge_slot(key, part):
    in_use, row_table, edge_key = route_plan(key)
    per_target = jnp.transpose(in_use, (1, 0, 2)).reshape(PEERS, PEERS * CAP)
    target_keys = jax.random.split(edge_key, PEERS)
    slot_table = jax.vmap(edges_for)(per_target, target_keys)
    return slot_table.reshape(-1).astype(jnp.int32)


def set_ends(entries, rng, low, largest):
    longest = entries.shape.index(max(entries.shape))
    spots = []
    for shift in (0, 1):
        where = [jax.random.randint(jax.random.fold_in(rng, axis), (), 0, length) for axis, length in enumerate(entries.shape)]
        where[longest] = (where[longest] + shift) % entries.shape[longest]
        spots.append(tuple(where))
    return entries.at[spots[0]].set(low).at[spots[1]].set(largest)


def shard_levels(rng, dims, pieces, least, top_value):
    def one(dim, shards_of):
        draws = jax.random.uniform(jax.random.fold_in(jax.random.fold_in(rng, 6), dim), (shards_of,), jnp.float32, least / len(pieces), top_value / len(pieces))
        return jnp.repeat(jnp.exp(draws), dims[dim] // shards_of).reshape((-1,) + (1,) * (len(dims) - dim - 1))

    factor_of = one(*pieces[0])
    for cut in pieces[1:]:
        factor_of = factor_of * one(*cut)
    return factor_of


def centred(rng, dims, scale, bound, cuts=(), kind=jnp.bfloat16):
    entries = jax.random.normal(rng, dims, jnp.float32) * scale
    if len(cuts) > 0:
        entries = shard_levels(rng, dims, cuts, -0.22, 0.18) * entries
    return jnp.clip(entries, min=-bound, max=bound).astype(kind)


def setup_inputs(seed: int = 0) -> dict:
    keys = jax.random.split(jax.random.key(seed), 14)
    return {
        "node_latents": centred(keys[0], (NODES, D), 1.0, 6.0, ((0, 8),)),
        "edge_latents": centred(keys[1], (EDGES, D), 1.0, 6.0, ((0, 8),)),
        "send_rows": draw_send_rows(jax.random.fold_in(keys[13], 71), 0),
        "edge_slot": draw_edge_slot(jax.random.fold_in(keys[13], 71), 0),
        "receivers": set_ends(jax.random.randint(keys[4], (EDGES,), 0, NODE_DEV), jax.random.fold_in(keys[4], 1), 0, NODE_DEV - 1).astype(jnp.int32),
        "edge_in_w": centred(keys[5], (LAYERS, 3, D, H), (3 * D) ** -0.5, 0.15625, ((3, 4),)),
        "edge_in_b": centred(keys[6], (LAYERS, H), 0.5, 3.0, ((1, 4),), jnp.float32),
        "edge_out_w": centred(keys[7], (LAYERS, H, D), H ** -0.5, 0.25, ((1, 4),)),
        "edge_gain": jnp.clip(jnp.exp(jax.random.uniform(keys[8], (LAYERS, D), jnp.float32, math.log(0.5), math.log(2.0))), 0.5, 2.0),
        "node_in_w": centred(keys[9], (LAYERS, 2, D, H), (2 * D) ** -0.5, 0.1875, ((3, 4),)),
        "node_in_b": centred(keys[10], (LAYERS, H), 0.5, 3.0, ((1, 4),), jnp.float32),
        "node_out_w": centred(keys[11], (LAYERS, H, D), H ** -0.5, 0.25, ((1, 4),)),
        "node_gain": jnp.clip(jnp.exp(jax.random.uniform(keys[12], (LAYERS, D), jnp.float32, math.log(0.5), math.log(2.0))), 0.5, 2.0),
    }


def layer_norm(values, scales):
    center = values - lax.optimization_barrier(jnp.mean(values, axis=-1, keepdims=True))
    spread = lax.optimization_barrier(jnp.mean(center * center, axis=-1, keepdims=True))
    return center * lax.rsqrt(spread + 1e-05) * scales

def split_sum(hidden, weight):
    share_width = weight.shape[0] // N_FEAT
    running = jnp.zeros((hidden.shape[0], weight.shape[1]), jnp.float32)
    for feat_idx in range(N_FEAT):
        first = feat_idx * share_width
        partial_value = jnp.dot(hidden[:, first:first + share_width], weight[first:first + share_width], preferred_element_type=jnp.float32)
        rounded = lax.optimization_barrier(partial_value.astype(jnp.bfloat16))
        running = running + rounded.astype(jnp.float32)
    return running

def reference(node_latents, edge_latents, send_rows, edge_slot, receivers, edge_in_w, edge_in_b, edge_out_w, edge_gain, node_in_w, node_in_b, node_out_w, node_gain):
    slot_table = edge_slot.reshape(PEERS, EDGE_DEV)
    source = (slot_table // CAP).astype(jnp.int32)
    offset = (slot_table % CAP).astype(jnp.int32)
    target = jnp.arange(PEERS, dtype=jnp.int32)[:, None]
    local_rows = send_rows[source, target, offset]
    senders = (source * NODE_DEV + local_rows).reshape(-1).astype(jnp.int32)
    targets = (target * NODE_DEV + receivers.reshape(PEERS, EDGE_DEV)).reshape(-1).astype(jnp.int32)
    node_state = node_latents
    edge_state = edge_latents
    for layer_idx in range(LAYERS):
        sender_proj = jnp.dot(node_state, edge_in_w[layer_idx, 1], preferred_element_type=jnp.float32).astype(jnp.bfloat16)
        receiver_proj = jnp.dot(node_state, edge_in_w[layer_idx, 2], preferred_element_type=jnp.float32).astype(jnp.bfloat16)
        preact = jnp.dot(edge_state, edge_in_w[layer_idx, 0], preferred_element_type=jnp.float32)
        preact = preact + sender_proj[senders].astype(jnp.float32) + receiver_proj[targets].astype(jnp.float32) + edge_in_b[layer_idx]
        edge_hidden = jax.nn.silu(preact).astype(jnp.bfloat16)
        message = layer_norm(split_sum(edge_hidden, edge_out_w[layer_idx]), edge_gain[layer_idx])
        update = message.astype(jnp.bfloat16)
        edge_next = (edge_state.astype(jnp.float32) + message).astype(jnp.bfloat16)
        incoming = jax.ops.segment_sum(update.astype(jnp.float32), targets, num_segments=PEERS * NODE_DEV).astype(jnp.bfloat16)
        node_pre = jnp.dot(node_state, node_in_w[layer_idx, 0], preferred_element_type=jnp.float32)
        node_pre = node_pre + jnp.dot(incoming, node_in_w[layer_idx, 1], preferred_element_type=jnp.float32) + node_in_b[layer_idx]
        node_hidden = jax.nn.silu(node_pre).astype(jnp.bfloat16)
        node_change = layer_norm(split_sum(node_hidden, node_out_w[layer_idx]), node_gain[layer_idx])
        node_state = (node_state.astype(jnp.float32) + node_change).astype(jnp.bfloat16)
        edge_state = edge_next
    return (node_state, edge_state)
```

```python
import functools

import jax
import jax.numpy as jnp
from jax import lax
from jax.experimental import pallas as pl
from jax.experimental.pallas import tpu as pltpu
from jax.sharding import PartitionSpec as P

BF = jnp.bfloat16
F32 = jnp.float32
MESH = pl.DeviceIdType.MESH
BLOCK = 256
LANES = 128


def silu(v):
    return v * (0.5 + 0.5 * jnp.tanh(0.5 * v))


def norm(v, gain):
    center = v - jnp.mean(v, axis=-1, keepdims=True)
    spread = jnp.mean(center * center, axis=-1, keepdims=True)
    return center * lax.rsqrt(spread + 1e-05) * gain


def dot(a, b):
    return jnp.dot(a, b, preferred_element_type=F32)


def kernel(
    patches,
    feats,
    nodes_in,
    edges_in,
    send_rows,
    slots,
    recvs,
    ein,
    eb,
    eo,
    egain,
    nin,
    nb,
    no,
    ngain,
    nodes_out,
    edges_out,
    own_b,
    all_b,
    w_send,
    w_edge,
    w_eo,
    w_nin,
    w_no,
    table,
    hot_slot,
    hot_recv,
    hot_recv_t,
    hot_send,
    edge,
    pre,
    upd,
    node,
    proj,
    picked,
    part,
    other,
    rproj,
    sem_in,
    sem_loc,
    sem_ys,
    sem_yr,
    sem_cs,
    sem_cr,
    sem_bs,
    sem_br,
    sem_ts,
    sem_tr,
    sem_fs,
    sem_fr,
    sem_ps,
    sem_pr,
    sem_os,
    sem_or,
    sem_ol,
):
    layers = ein.shape[0]
    me = lax.axis_index("patch")
    f = lax.axis_index("feat")
    core = lax.rem(f, 2)
    mate = f + 1 - 2 * core
    half_feats = feats // 2
    width = ein.shape[3]
    half_width = half_feats * width
    cap = send_rows.shape[1]
    half = edge.shape[0]
    nrows = node.shape[0]
    blocks = half // BLOCK

    def place(q):
        return lax.rem(q, 2) * half_feats + q // 2

    def cols(q):
        return pl.ds(pl.multiple_of(place(q) * width, width), width)

    def source(k):
        l, i = divmod(k, 6)
        return (ein.at[l, 1], ein.at[l, 0], ein.at[l, 2], eo.at[l], nin.at[l], no.at[l])[i]

    def target(k, q):
        l, i = divmod(k, 6)
        if i == 0:
            return w_send.at[l, :, pl.ds(pl.multiple_of(q // 2 * width, width), width)]
        if i in (1, 2):
            return w_edge.at[l, i - 1, :, cols(q)]
        if i == 3:
            return w_eo.at[l, cols(q), :]
        if i == 4:
            return w_nin.at[l, :, :, cols(q)]
        return w_no.at[l, cols(q), :]

    def remote(src, dst, ss, rs, **where):
        return pltpu.make_async_remote_copy(
            src_ref=src, dst_ref=dst, send_sem=ss, recv_sem=rs, device_id=where, device_id_type=MESH
        )

    def local_copy(k):
        return pltpu.make_async_copy(source(k), target(k, f), sem_loc.at[k])

    def across(k, j, q):
        return remote(
            source(k), target(k, q), sem_ys.at[k, j], sem_yr.at[k, j],
            feat=lax.rem(f + 2 * j, feats),
        )

    def beside(k, j, q):
        src = source(k) if j == 0 else target(k, q)
        return remote(src, target(k, q), sem_cs.at[k, j], sem_cr.at[k, j], feat=mate)

    def back(q, j):
        return lax.rem(q + feats - 2 * j, feats)

    def start_weights(l):
        for k in range(6 * l, 6 * l + 6):
            for j in range(1, half_feats):
                across(k, j, f).start()
            local_copy(k).start()
            if k % 6:
                beside(k, 0, f).start()

    def advance(k):
        for j in range(1, half_feats):
            across(k, j, back(f, j)).wait_recv()
            if k % 6:
                beside(k, j, back(f, j)).start()

    def acquire(k):
        local_copy(k).wait()
        if k % 6:
            for j in range(half_feats):
                beside(k, j, back(mate, j)).wait_recv()

    def bias_copy(j, q):
        return remote(
            own_b, all_b.at[q], sem_bs.at[j], sem_br.at[j], feat=lax.rem(f + j, feats)
        )

    barrier = pltpu.get_barrier_semaphore()
    for j in range(1, feats):
        pl.semaphore_signal(
            barrier, inc=1, device_id={"feat": lax.rem(f + j, feats)}, device_id_type=MESH
        )

    def greet(j, carry):
        pl.semaphore_signal(
            barrier, inc=1, device_id={"patch": lax.rem(me + j, patches)}, device_id_type=MESH
        )
        return carry

    lax.fori_loop(1, patches, greet, 0)
    load_nodes = pltpu.make_async_copy(nodes_in, node, sem_in.at[0])
    load_edges = pltpu.make_async_copy(
        edges_in.at[pl.ds(pl.multiple_of(core * half, half), half)], edge, sem_in.at[1]
    )
    load_nodes.start()
    load_edges.start()
    own_b[...] = jnp.zeros_like(own_b)
    own_b[0:layers] = eb[...]
    own_b[layers : 2 * layers] = nb[...]
    all_b[f] = own_b[...]
    pl.semaphore_wait(barrier, feats - 1 + patches - 1)
    for j in range(1, feats):
        bias_copy(j, f).start()
    start_weights(0)

    lines = half // LANES
    first_line = core * lines

    def column(row):
        return jnp.transpose(jnp.broadcast_to(row, (LANES, LANES)))

    def spread_hot(ref, row0, col):
        for c in range(ref.shape[1] // LANES):
            ids = lax.broadcasted_iota(jnp.int32, (LANES, LANES), 1) + c * LANES
            ref[pl.ds(row0, LANES), c * LANES : (c + 1) * LANES] = jnp.where(
                ids == col, 1.0, 0.0
            ).astype(BF)

    def build_send(i, carry):
        spread_hot(hot_send, pl.multiple_of(i * LANES, LANES), column(send_rows[pl.ds(i, 1), :]))
        return carry

    lax.fori_loop(0, patches, build_send, 0)

    def build_edge(i, carry):
        at = pl.multiple_of(i * LANES, LANES)
        row = recvs[pl.ds(first_line + i, 1), :]
        ids = lax.broadcasted_iota(jnp.int32, (nrows, LANES), 0)
        hot_recv_t[:, pl.ds(at, LANES)] = jnp.where(ids == row, 1.0, 0.0).astype(BF)
        spread_hot(hot_recv, at, column(row))
        spread_hot(hot_slot, at, column(slots[pl.ds(first_line + i, 1), :]))
        return carry

    def table_copy(l, s, d):
        return remote(
            picked.at[pl.ds(pl.multiple_of(d * cap, cap), cap)],
            table.at[
                l,
                pl.ds(pl.multiple_of(s * cap, cap), cap),
                pl.ds(pl.multiple_of(core * half_width, half_width), half_width),
            ],
            sem_ts.at[l, d],
            sem_tr.at[l, s],
            patch=d,
        )

    def table_pass(l, s, c):
        part_of = table.at[
            l,
            pl.ds(pl.multiple_of(s * cap, cap), cap),
            pl.ds(pl.multiple_of(c * half_width, half_width), half_width),
        ]
        return remote(part_of, part_of, sem_fs.at[l, s], sem_fr.at[l, s], feat=mate)

    def bias(row):
        order = sorted(range(feats), key=lambda q: (q % 2) * half_feats + q // 2)
        return jnp.concatenate([all_b[q, row : row + 1, :] for q in order], axis=1)

    def out_local(b):
        rows = pl.ds(pl.multiple_of(b * BLOCK, BLOCK), BLOCK)
        dst = pl.ds(pl.multiple_of(core * half + b * BLOCK, BLOCK), BLOCK)
        return pltpu.make_async_copy(edge.at[rows], edges_out.at[dst], sem_ol.at[b])

    def out_remote(b, c):
        rows = pl.ds(pl.multiple_of(b * BLOCK, BLOCK), BLOCK)
        dst = pl.ds(pl.multiple_of(c * half + b * BLOCK, BLOCK), BLOCK)
        return remote(edge.at[rows], edges_out.at[dst], sem_os.at[b], sem_or.at[b], feat=mate)

    load_nodes.wait()
    for l in range(layers):
        k0 = 6 * l
        advance(k0)
        acquire(k0)
        proj[...] = dot(node[...], w_send[l]).astype(BF)

        def pick(j, carry, l=l):
            d = lax.rem(me + j, patches)
            rows = pl.ds(pl.multiple_of(d * cap, cap), cap)
            picked[rows, :] = dot(hot_send[rows, :], proj[...]).astype(BF)
            table_copy(l, me, d).start()
            return carry

        lax.fori_loop(1, patches, pick, 0)
        mine = pl.ds(pl.multiple_of(me * cap, cap), cap)
        table[
            l, mine, pl.ds(pl.multiple_of(core * half_width, half_width), half_width)
        ] = dot(hot_send[mine, :], proj[...]).astype(BF)
        table_pass(l, me, core).start()
        if l == 0:
            lax.fori_loop(0, lines, build_edge, 0)
            load_edges.wait()
            for j in range(1, feats):
                bias_copy(j, lax.rem(f + feats - j, feats)).wait_recv()
        advance(k0 + 1)
        advance(k0 + 2)
        acquire(k0 + 1)
        acquire(k0 + 2)
        for b in range(nrows // BLOCK):
            rows = slice(b * BLOCK, (b + 1) * BLOCK)
            rproj[rows] = dot(node[rows], w_edge[l, 1]).astype(BF)
        eb_row = bias(l)

        def begin(b, carry, l=l, eb_row=eb_row):
            rows = pl.ds(pl.multiple_of(b * BLOCK, BLOCK), BLOCK)
            pre[rows, :] = (
                dot(edge[rows, :], w_edge[l, 0]) + dot(hot_recv[rows, :], rproj[...]) + eb_row
            )
            return carry

        lax.fori_loop(0, blocks, begin, 0)

        def relay(j, carry, l=l):
            s = lax.rem(me + j, patches)
            table_copy(l, s, me).wait_recv()
            table_pass(l, s, core).start()
            return carry

        lax.fori_loop(1, patches, relay, 0)
        advance(k0 + 3)

        def settle(s, carry, l=l):
            table_pass(l, s, 1 - core).wait_recv()
            return carry

        lax.fori_loop(0, patches, settle, 0)
        acquire(k0 + 3)
        if l + 1 < layers:
            start_weights(l + 1)

        def work(b, carry, l=l):
            rows = pl.ds(pl.multiple_of(b * BLOCK, BLOCK), BLOCK)
            hidden = silu(pre[rows, :] + dot(hot_slot[rows, :], table[l])).astype(BF)
            message = norm(dot(hidden, w_eo[l]), egain[l : l + 1, :])
            upd[rows, :] = message.astype(BF)
            edge[rows, :] = (edge[rows, :].astype(F32) + message).astype(BF)
            if l == layers - 1:
                out_local(b).start()
                out_remote(b, core).start()
            return carry

        lax.fori_loop(0, blocks, work, 0)
        for b in range(nrows // BLOCK):
            rows = slice(b * BLOCK, (b + 1) * BLOCK)
            part[rows] = dot(hot_recv_t[rows, :], upd[...]).astype(BF)
        swap = remote(part, other.at[l], sem_ps.at[l], sem_pr.at[l], feat=mate)
        swap.start()
        advance(k0 + 4)
        advance(k0 + 5)
        acquire(k0 + 4)
        acquire(k0 + 5)
        swap.wait()
        nb_row = bias(layers + l)
        for b in range(nrows // BLOCK):
            rows = slice(b * BLOCK, (b + 1) * BLOCK)
            incoming = (part[rows].astype(F32) + other[l, rows].astype(F32)).astype(BF)
            hidden = silu(
                dot(node[rows], w_nin[l, 0]) + dot(incoming, w_nin[l, 1]) + nb_row
            ).astype(BF)
            change = norm(dot(hidden, w_no[l]), ngain[l : l + 1, :])
            node[rows] = (node[rows].astype(F32) + change).astype(BF)

        def drain(j, carry, l=l):
            table_copy(l, me, lax.rem(me + j, patches)).wait_send()
            return carry

        lax.fori_loop(1, patches, drain, 0)

    store_nodes = pltpu.make_async_copy(node, nodes_out, sem_in.at[2])
    store_nodes.start()
    for j in range(1, feats):
        bias_copy(j, f).wait_send()
    for k in range(6 * layers):
        for j in range(1, half_feats):
            across(k, j, f).wait_send()
        if k % 6:
            for j in range(half_feats):
                beside(k, j, back(f, j)).wait_send()
    for l in range(layers):

        def done(s, carry, l=l):
            table_pass(l, s, core).wait_send()
            return carry

        lax.fori_loop(0, patches, done, 0)

    def finish(b, carry):
        out_local(b).wait()
        out_remote(b, core).wait_send()
        out_remote(b, 1 - core).wait_recv()
        return carry

    lax.fori_loop(0, blocks, finish, 0)
    store_nodes.wait()


def body(patches, feats, *args):
    (nodes, edges, send_rows, edge_slot, receivers, ein, eb, eo, egain, nin, nb, no, ngain) = args
    layers = ein.shape[0]
    nrows, dim = nodes.shape
    erows = edges.shape[0]
    half = erows // 2
    width = ein.shape[3]
    hid = width * feats
    cap = send_rows.shape[2]
    slots = patches * cap
    blocks = half // BLOCK
    vmem = pltpu.VMEM
    bias_rows = -(-2 * layers // 8) * 8
    dma = pltpu.SemaphoreType.DMA
    any_spec = pl.BlockSpec(memory_space=pl.ANY)
    v_spec = pl.BlockSpec(memory_space=vmem)
    call = pl.pallas_call(
        functools.partial(kernel, patches, feats),
        out_shape=(
            jax.ShapeDtypeStruct((nrows, dim), BF),
            jax.ShapeDtypeStruct((erows, dim), BF),
        ),
        in_specs=[
            any_spec, any_spec, v_spec, v_spec, v_spec, any_spec, v_spec, any_spec, v_spec,
            any_spec, v_spec, any_spec, v_spec,
        ],
        out_specs=(any_spec, any_spec),
        scratch_shapes=[
            vmem((bias_rows, width), F32),
            vmem((feats, bias_rows, width), F32),
            vmem((layers, dim, hid // 2), BF),
            vmem((layers, 2, dim, hid), BF),
            vmem((layers, hid, dim), BF),
            vmem((layers, 2, dim, hid), BF),
            vmem((layers, hid, dim), BF),
            vmem((layers, slots, hid), BF),
            vmem((half, slots), BF),
            vmem((half, nrows), BF),
            vmem((nrows, half), BF),
            vmem((slots, nrows), BF),
            vmem((half, dim), BF),
            vmem((half, hid), F32),
            vmem((half, dim), BF),
            vmem((nrows, dim), BF),
            vmem((nrows, hid // 2), BF),
            vmem((slots, hid // 2), BF),
            vmem((nrows, dim), BF),
            vmem((layers, nrows, dim), BF),
            vmem((nrows, hid), BF),
            dma((3,)),
            dma((6 * layers,)),
            dma((6 * layers, feats // 2)),
            dma((6 * layers, feats // 2)),
            dma((6 * layers, feats // 2)),
            dma((6 * layers, feats // 2)),
            dma((feats,)),
            dma((feats,)),
            dma((layers, patches)),
            dma((layers, patches)),
            dma((layers, patches)),
            dma((layers, patches)),
            dma((layers,)),
            dma((layers,)),
            dma((blocks,)),
            dma((blocks,)),
            dma((blocks,)),
        ],
        compiler_params=pltpu.CompilerParams(
            collective_id=0, has_side_effects=True, vmem_limit_bytes=62 * 2**20
        ),
    )
    return call(
        nodes,
        edges,
        send_rows.reshape(patches, cap),
        edge_slot.reshape(erows // LANES, LANES),
        receivers.reshape(erows // LANES, LANES),
        ein, eb, eo, egain, nin, nb, no, ngain,
    )


def solution(mesh):
    in_specs = (
        P("patch", None),
        P("patch", None),
        P("patch", None, None),
        P("patch"),
        P("patch"),
        P(None, None, None, "feat"),
        P(None, "feat"),
        P(None, "feat", None),
        P(),
        P(None, None, None, "feat"),
        P(None, "feat"),
        P(None, "feat", None),
        P(),
    )
    out_specs = (P("patch", None), P("patch", None))
    inner = functools.partial(body, mesh.shape["patch"], mesh.shape["feat"])
    return jax.shard_map(inner, mesh=mesh, in_specs=in_specs, out_specs=out_specs, check_vma=False)
```

```python
import functools

import jax
import jax.numpy as jnp
from jax import lax
from jax.experimental import pallas as pl
from jax.experimental.pallas import tpu as pltpu
from jax.sharding import PartitionSpec as P

BF = jnp.bfloat16
F32 = jnp.float32
MESH = pl.DeviceIdType.MESH
BLOCK = 256
LANES = 128


def silu(v):
    return v * (0.5 + 0.5 * jnp.tanh(0.5 * v))


def norm(v, gain):
    center = v - jnp.mean(v, axis=-1, keepdims=True)
    spread = jnp.mean(center * center, axis=-1, keepdims=True)
    return center * lax.rsqrt(spread + 1e-05) * gain


def dot(a, b):
    return jnp.dot(a, b, preferred_element_type=F32)


def kernel(
    patches,
    feats,
    nodes_in,
    edges_in,
    send_rows,
    slots,
    recvs,
    ein,
    eb,
    eo,
    egain,
    nin,
    nb,
    no,
    ngain,
    nodes_out,
    edges_out,
    own_b,
    all_b,
    w_send,
    w_edge,
    w_eo,
    w_nin,
    w_no,
    table,
    hot_slot,
    hot_recv,
    hot_recv_t,
    hot_send,
    edge,
    pre,
    upd,
    node,
    proj,
    picked,
    part,
    other,
    rproj,
    sem_in,
    sem_loc,
    sem_ys,
    sem_yr,
    sem_cs,
    sem_cr,
    sem_bs,
    sem_br,
    sem_ts,
    sem_tr,
    sem_fs,
    sem_fr,
    sem_ps,
    sem_pr,
    sem_os,
    sem_or,
    sem_ol,
):
    layers = ein.shape[0]
    me = lax.axis_index("patch")
    f = lax.axis_index("feat")
    core = lax.rem(f, 2)
    mate = f + 1 - 2 * core
    half_feats = feats // 2
    width = ein.shape[3]
    half_width = half_feats * width
    cap = send_rows.shape[1]
    half = edge.shape[0]
    nrows = node.shape[0]
    blocks = half // BLOCK

    def place(q):
        return lax.rem(q, 2) * half_feats + q // 2

    def cols(q):
        return pl.ds(pl.multiple_of(place(q) * width, width), width)

    def source(k):
        l, i = divmod(k, 6)
        return (ein.at[l, 1], ein.at[l, 0], ein.at[l, 2], eo.at[l], nin.at[l], no.at[l])[i]

    def target(k, q):
        l, i = divmod(k, 6)
        if i == 0:
            return w_send.at[l, :, pl.ds(pl.multiple_of(q // 2 * width, width), width)]
        if i in (1, 2):
            return w_edge.at[l, i - 1, :, cols(q)]
        if i == 3:
            return w_eo.at[l, cols(q), :]
        if i == 4:
            return w_nin.at[l, :, :, cols(q)]
        return w_no.at[l, cols(q), :]

    def remote(src, dst, ss, rs, **where):
        return pltpu.make_async_remote_copy(
            src_ref=src, dst_ref=dst, send_sem=ss, recv_sem=rs, device_id=where, device_id_type=MESH
        )

    def local_copy(k):
        return pltpu.make_async_copy(source(k), target(k, f), sem_loc.at[k])

    def across(k, j, q):
        return remote(
            source(k), target(k, q), sem_ys.at[k, j], sem_yr.at[k, j],
            feat=lax.rem(f + 2 * j, feats),
        )

    def beside(k, j, q):
        src = source(k) if j == 0 else target(k, q)
        return remote(src, target(k, q), sem_cs.at[k, j], sem_cr.at[k, j], feat=mate)

    def back(q, j):
        return lax.rem(q + feats - 2 * j, feats)

    def start_weights(l):
        for k in range(6 * l, 6 * l + 6):
            for j in range(1, half_feats):
                across(k, j, f).start()
            local_copy(k).start()
            if k % 6:
                beside(k, 0, f).start()

    def advance(k):
        for j in range(1, half_feats):
            across(k, j, back(f, j)).wait_recv()
            if k % 6:
                beside(k, j, back(f, j)).start()

    def acquire(k):
        local_copy(k).wait()
        if k % 6:
            for j in range(half_feats):
                beside(k, j, back(mate, j)).wait_recv()

    def bias_copy(j, q):
        return remote(
            own_b, all_b.at[q], sem_bs.at[j], sem_br.at[j], feat=lax.rem(f + j, feats)
        )

    barrier = pltpu.get_barrier_semaphore()
    for j in range(1, feats):
        pl.semaphore_signal(
            barrier, inc=1, device_id={"feat": lax.rem(f + j, feats)}, device_id_type=MESH
        )

    def greet(j, carry):
        pl.semaphore_signal(
            barrier, inc=1, device_id={"patch": lax.rem(me + j, patches)}, device_id_type=MESH
        )
        return carry

    lax.fori_loop(1, patches, greet, 0)
    load_nodes = pltpu.make_async_copy(nodes_in, node, sem_in.at[0])
    load_edges = pltpu.make_async_copy(
        edges_in.at[pl.ds(pl.multiple_of(core * half, half), half)], edge, sem_in.at[1]
    )
    load_nodes.start()
    load_edges.start()
    own_b[...] = jnp.zeros_like(own_b)
    own_b[0:layers] = eb[...]
    own_b[layers : 2 * layers] = nb[...]
    all_b[f] = own_b[...]
    pl.semaphore_wait(barrier, feats - 1 + patches - 1)
    for j in range(1, feats):
        bias_copy(j, f).start()
    start_weights(0)

    lines = half // LANES
    first_line = core * lines

    def column(row):
        return jnp.transpose(jnp.broadcast_to(row, (LANES, LANES)))

    def spread_hot(ref, row0, col):
        for c in range(ref.shape[1] // LANES):
            ids = lax.broadcasted_iota(jnp.int32, (LANES, LANES), 1) + c * LANES
            ref[pl.ds(row0, LANES), c * LANES : (c + 1) * LANES] = jnp.where(
                ids == col, 1.0, 0.0
            ).astype(BF)

    def build_send(i, carry):
        spread_hot(hot_send, pl.multiple_of(i * LANES, LANES), column(send_rows[pl.ds(i, 1), :]))
        return carry

    lax.fori_loop(0, patches, build_send, 0)

    def build_edge(i, carry):
        at = pl.multiple_of(i * LANES, LANES)
        row = recvs[pl.ds(first_line + i, 1), :]
        ids = lax.broadcasted_iota(jnp.int32, (nrows, LANES), 0)
        hot_recv_t[:, pl.ds(at, LANES)] = jnp.where(ids == row, 1.0, 0.0).astype(BF)
        spread_hot(hot_recv, at, column(row))
        spread_hot(hot_slot, at, column(slots[pl.ds(first_line + i, 1), :]))
        return carry

    def table_copy(l, s, d):
        return remote(
            picked.at[pl.ds(pl.multiple_of(d * cap, cap), cap)],
            table.at[
                l,
                pl.ds(pl.multiple_of(s * cap, cap), cap),
                pl.ds(pl.multiple_of(core * half_width, half_width), half_width),
            ],
            sem_ts.at[l, d],
            sem_tr.at[l, s],
            patch=d,
        )

    def table_pass(l, s, c):
        part_of = table.at[
            l,
            pl.ds(pl.multiple_of(s * cap, cap), cap),
            pl.ds(pl.multiple_of(c * half_width, half_width), half_width),
        ]
        return remote(part_of, part_of, sem_fs.at[l, s], sem_fr.at[l, s], feat=mate)

    def bias(row):
        order = sorted(range(feats), key=lambda q: (q % 2) * half_feats + q // 2)
        return jnp.concatenate([all_b[q, row : row + 1, :] for q in order], axis=1)

    def out_local(b):
        rows = pl.ds(pl.multiple_of(b * BLOCK, BLOCK), BLOCK)
        dst = pl.ds(pl.multiple_of(core * half + b * BLOCK, BLOCK), BLOCK)
        return pltpu.make_async_copy(edge.at[rows], edges_out.at[dst], sem_ol.at[b])

    def out_remote(b, c):
        rows = pl.ds(pl.multiple_of(b * BLOCK, BLOCK), BLOCK)
        dst = pl.ds(pl.multiple_of(c * half + b * BLOCK, BLOCK), BLOCK)
        return remote(edge.at[rows], edges_out.at[dst], sem_os.at[b], sem_or.at[b], feat=mate)

    load_nodes.wait()
    for l in range(layers):
        k0 = 6 * l
        advance(k0)
        acquire(k0)
        proj[...] = dot(node[...], w_send[l]).astype(BF)

        def pick(j, carry, l=l):
            d = lax.rem(me + j, patches)
            rows = pl.ds(pl.multiple_of(d * cap, cap), cap)
            picked[rows, :] = dot(hot_send[rows, :], proj[...]).astype(BF)
            table_copy(l, me, d).start()
            return carry

        lax.fori_loop(1, patches, pick, 0)
        mine = pl.ds(pl.multiple_of(me * cap, cap), cap)
        table[
            l, mine, pl.ds(pl.multiple_of(core * half_width, half_width), half_width)
        ] = dot(hot_send[mine, :], proj[...]).astype(BF)
        table_pass(l, me, core).start()
        if l == 0:
            lax.fori_loop(0, lines, build_edge, 0)
            load_edges.wait()
            for j in range(1, feats):
                bias_copy(j, lax.rem(f + feats - j, feats)).wait_recv()
        advance(k0 + 1)
        advance(k0 + 2)
        acquire(k0 + 1)
        acquire(k0 + 2)
        for b in range(nrows // BLOCK):
            rows = slice(b * BLOCK, (b + 1) * BLOCK)
            rproj[rows] = dot(node[rows], w_edge[l, 1]).astype(BF)
        eb_row = bias(l)

        def begin(b, carry, l=l, eb_row=eb_row):
            rows = pl.ds(pl.multiple_of(b * BLOCK, BLOCK), BLOCK)
            pre[rows, :] = (
                dot(edge[rows, :], w_edge[l, 0]) + dot(hot_recv[rows, :], rproj[...]) + eb_row
            )
            return carry

        lax.fori_loop(0, blocks, begin, 0)

        def relay(j, carry, l=l):
            s = lax.rem(me + j, patches)
            table_copy(l, s, me).wait_recv()
            table_pass(l, s, core).start()
            return carry

        lax.fori_loop(1, patches, relay, 0)
        advance(k0 + 3)

        def settle(s, carry, l=l):
            table_pass(l, s, 1 - core).wait_recv()
            return carry

        lax.fori_loop(0, patches, settle, 0)
        acquire(k0 + 3)
        if l + 1 < layers:
            start_weights(l + 1)

        def first(b, l=l):
            rows = pl.ds(pl.multiple_of(b * BLOCK, BLOCK), BLOCK)
            upd[rows, :] = silu(pre[rows, :] + dot(hot_slot[rows, :], table[l])).astype(BF)

        def second(b, l=l):
            rows = pl.ds(pl.multiple_of(b * BLOCK, BLOCK), BLOCK)
            message = norm(dot(upd[rows, :], w_eo[l]), egain[l : l + 1, :])
            upd[rows, :] = message.astype(BF)
            edge[rows, :] = (edge[rows, :].astype(F32) + message).astype(BF)

        def hand_out(b, l=l):
            if l == layers - 1:
                out_local(b).start()
                out_remote(b, core).start()

        def work(b, carry):
            second(b - 1)
            first(b)
            hand_out(b - 1)
            return carry

        first(0)
        lax.fori_loop(1, blocks, work, 0)
        second(blocks - 1)
        hand_out(blocks - 1)
        for b in range(nrows // BLOCK):
            rows = slice(b * BLOCK, (b + 1) * BLOCK)
            part[rows] = dot(hot_recv_t[rows, :], upd[...]).astype(BF)
        swap = remote(part, other.at[l], sem_ps.at[l], sem_pr.at[l], feat=mate)
        swap.start()
        advance(k0 + 4)
        advance(k0 + 5)
        acquire(k0 + 4)
        acquire(k0 + 5)
        swap.wait()
        nb_row = bias(layers + l)
        for b in range(nrows // BLOCK):
            rows = slice(b * BLOCK, (b + 1) * BLOCK)
            incoming = (part[rows].astype(F32) + other[l, rows].astype(F32)).astype(BF)
            hidden = silu(
                dot(node[rows], w_nin[l, 0]) + dot(incoming, w_nin[l, 1]) + nb_row
            ).astype(BF)
            change = norm(dot(hidden, w_no[l]), ngain[l : l + 1, :])
            node[rows] = (node[rows].astype(F32) + change).astype(BF)

        def drain(j, carry, l=l):
            table_copy(l, me, lax.rem(me + j, patches)).wait_send()
            return carry

        lax.fori_loop(1, patches, drain, 0)

    store_nodes = pltpu.make_async_copy(node, nodes_out, sem_in.at[2])
    store_nodes.start()
    for j in range(1, feats):
        bias_copy(j, f).wait_send()
    for k in range(6 * layers):
        for j in range(1, half_feats):
            across(k, j, f).wait_send()
        if k % 6:
            for j in range(half_feats):
                beside(k, j, back(f, j)).wait_send()
    for l in range(layers):

        def done(s, carry, l=l):
            table_pass(l, s, core).wait_send()
            return carry

        lax.fori_loop(0, patches, done, 0)

    def finish(b, carry):
        out_local(b).wait()
        out_remote(b, core).wait_send()
        out_remote(b, 1 - core).wait_recv()
        return carry

    lax.fori_loop(0, blocks, finish, 0)
    store_nodes.wait()


def body(patches, feats, *args):
    (nodes, edges, send_rows, edge_slot, receivers, ein, eb, eo, egain, nin, nb, no, ngain) = args
    layers = ein.shape[0]
    nrows, dim = nodes.shape
    erows = edges.shape[0]
    half = erows // 2
    width = ein.shape[3]
    hid = width * feats
    cap = send_rows.shape[2]
    slots = patches * cap
    blocks = half // BLOCK
    vmem = pltpu.VMEM
    bias_rows = -(-2 * layers // 8) * 8
    dma = pltpu.SemaphoreType.DMA
    any_spec = pl.BlockSpec(memory_space=pl.ANY)
    v_spec = pl.BlockSpec(memory_space=vmem)
    call = pl.pallas_call(
        functools.partial(kernel, patches, feats),
        out_shape=(
            jax.ShapeDtypeStruct((nrows, dim), BF),
            jax.ShapeDtypeStruct((erows, dim), BF),
        ),
        in_specs=[
            any_spec, any_spec, v_spec, v_spec, v_spec, any_spec, v_spec, any_spec, v_spec,
            any_spec, v_spec, any_spec, v_spec,
        ],
        out_specs=(any_spec, any_spec),
        scratch_shapes=[
            vmem((bias_rows, width), F32),
            vmem((feats, bias_rows, width), F32),
            vmem((layers, dim, hid // 2), BF),
            vmem((layers, 2, dim, hid), BF),
            vmem((layers, hid, dim), BF),
            vmem((layers, 2, dim, hid), BF),
            vmem((layers, hid, dim), BF),
            vmem((layers, slots, hid), BF),
            vmem((half, slots), BF),
            vmem((half, nrows), BF),
            vmem((nrows, half), BF),
            vmem((slots, nrows), BF),
            vmem((half, dim), BF),
            vmem((half, hid), F32),
            vmem((half, dim), BF),
            vmem((nrows, dim), BF),
            vmem((nrows, hid // 2), BF),
            vmem((slots, hid // 2), BF),
            vmem((nrows, dim), BF),
            vmem((layers, nrows, dim), BF),
            vmem((nrows, hid), BF),
            dma((3,)),
            dma((6 * layers,)),
            dma((6 * layers, feats // 2)),
            dma((6 * layers, feats // 2)),
            dma((6 * layers, feats // 2)),
            dma((6 * layers, feats // 2)),
            dma((feats,)),
            dma((feats,)),
            dma((layers, patches)),
            dma((layers, patches)),
            dma((layers, patches)),
            dma((layers, patches)),
            dma((layers,)),
            dma((layers,)),
            dma((blocks,)),
            dma((blocks,)),
            dma((blocks,)),
        ],
        compiler_params=pltpu.CompilerParams(
            collective_id=0, has_side_effects=True, vmem_limit_bytes=62 * 2**20
        ),
    )
    return call(
        nodes,
        edges,
        send_rows.reshape(patches, cap),
        edge_slot.reshape(erows // LANES, LANES),
        receivers.reshape(erows // LANES, LANES),
        ein, eb, eo, egain, nin, nb, no, ngain,
    )


def solution(mesh):
    in_specs = (
        P("patch", None),
        P("patch", None),
        P("patch", None, None),
        P("patch"),
        P("patch"),
        P(None, None, None, "feat"),
        P(None, "feat"),
        P(None, "feat", None),
        P(),
        P(None, None, None, "feat"),
        P(None, "feat"),
        P(None, "feat", None),
        P(),
    )
    out_specs = (P("patch", None), P("patch", None))
    inner = functools.partial(body, mesh.shape["patch"], mesh.shape["feat"])
    return jax.shard_map(inner, mesh=mesh, in_specs=in_specs, out_specs=out_specs, check_vma=False)
```

```python
import functools

import jax
import jax.numpy as jnp
from jax import lax
from jax.experimental import pallas as pl
from jax.experimental.pallas import tpu as pltpu
from jax.sharding import PartitionSpec as P

BF = jnp.bfloat16
F32 = jnp.float32
MESH = pl.DeviceIdType.MESH
BLOCK = 256
LANES = 128


def silu(v):
    return v * (0.5 + 0.5 * jnp.tanh(0.5 * v))


def norm(v, gain):
    center = v - jnp.mean(v, axis=-1, keepdims=True)
    spread = jnp.mean(center * center, axis=-1, keepdims=True)
    return center * lax.rsqrt(spread + 1e-05) * gain


def dot(a, b):
    return jnp.dot(a, b, preferred_element_type=F32)


def kernel(
    patches,
    feats,
    nodes_in,
    edges_in,
    send_rows,
    slots,
    recvs,
    ein,
    eb,
    eo,
    egain,
    nin,
    nb,
    no,
    ngain,
    nodes_out,
    edges_out,
    own_b,
    all_b,
    w_send,
    w_edge,
    w_eo,
    w_nin,
    w_no,
    table,
    hot_slot,
    hot_recv,
    hot_recv_t,
    hot_send,
    edge,
    pre,
    upd,
    node,
    proj,
    picked,
    part,
    other,
    rproj,
    sem_in,
    sem_loc,
    sem_ys,
    sem_yr,
    sem_cs,
    sem_cr,
    sem_bs,
    sem_br,
    sem_ts,
    sem_tr,
    sem_fs,
    sem_fr,
    sem_ps,
    sem_pr,
    sem_os,
    sem_or,
    sem_ol,
):
    layers = ein.shape[0]
    me = lax.axis_index("patch")
    f = lax.axis_index("feat")
    core = lax.rem(f, 2)
    mate = f + 1 - 2 * core
    half_feats = feats // 2
    width = ein.shape[3]
    half_width = half_feats * width
    cap = send_rows.shape[1]
    half = edge.shape[0]
    nrows = node.shape[0]
    blocks = half // BLOCK

    def place(q):
        return lax.rem(q, 2) * half_feats + q // 2

    def cols(q):
        return pl.ds(pl.multiple_of(place(q) * width, width), width)

    def source(k):
        l, i = divmod(k, 6)
        return (ein.at[l, 1], ein.at[l, 0], ein.at[l, 2], eo.at[l], nin.at[l], no.at[l])[i]

    def target(k, q):
        l, i = divmod(k, 6)
        if i == 0:
            return w_send.at[l, :, pl.ds(pl.multiple_of(q // 2 * width, width), width)]
        if i in (1, 2):
            return w_edge.at[l, i - 1, :, cols(q)]
        if i == 3:
            return w_eo.at[l, cols(q), :]
        if i == 4:
            return w_nin.at[l, :, :, cols(q)]
        return w_no.at[l, cols(q), :]

    def remote(src, dst, ss, rs, **where):
        return pltpu.make_async_remote_copy(
            src_ref=src, dst_ref=dst, send_sem=ss, recv_sem=rs, device_id=where, device_id_type=MESH
        )

    def local_copy(k):
        return pltpu.make_async_copy(source(k), target(k, f), sem_loc.at[k])

    def across(k, j, q):
        return remote(
            source(k), target(k, q), sem_ys.at[k, j], sem_yr.at[k, j],
            feat=lax.rem(f + 2 * j, feats),
        )

    def beside(k, j, q):
        src = source(k) if j == 0 else target(k, q)
        return remote(src, target(k, q), sem_cs.at[k, j], sem_cr.at[k, j], feat=mate)

    def back(q, j):
        return lax.rem(q + feats - 2 * j, feats)

    def start_weights(l):
        for k in range(6 * l, 6 * l + 6):
            for j in range(1, half_feats):
                across(k, j, f).start()
            local_copy(k).start()
            if k % 6:
                beside(k, 0, f).start()

    def advance(k):
        for j in range(1, half_feats):
            across(k, j, back(f, j)).wait_recv()
            if k % 6:
                beside(k, j, back(f, j)).start()

    def acquire(k):
        local_copy(k).wait()
        if k % 6:
            for j in range(half_feats):
                beside(k, j, back(mate, j)).wait_recv()

    def bias_copy(j, q):
        return remote(
            own_b, all_b.at[q], sem_bs.at[j], sem_br.at[j], feat=lax.rem(f + j, feats)
        )

    barrier = pltpu.get_barrier_semaphore()
    for j in range(1, feats):
        pl.semaphore_signal(
            barrier, inc=1, device_id={"feat": lax.rem(f + j, feats)}, device_id_type=MESH
        )

    def greet(j, carry):
        pl.semaphore_signal(
            barrier, inc=1, device_id={"patch": lax.rem(me + j, patches)}, device_id_type=MESH
        )
        return carry

    lax.fori_loop(1, patches, greet, 0)
    load_nodes = pltpu.make_async_copy(nodes_in, node, sem_in.at[0])
    load_edges = pltpu.make_async_copy(
        edges_in.at[pl.ds(pl.multiple_of(core * half, half), half)], edge, sem_in.at[1]
    )
    load_nodes.start()
    load_edges.start()
    own_b[...] = jnp.zeros_like(own_b)
    own_b[0:layers] = eb[...]
    own_b[layers : 2 * layers] = nb[...]
    all_b[f] = own_b[...]
    pl.semaphore_wait(barrier, feats - 1 + patches - 1)
    for j in range(1, feats):
        bias_copy(j, f).start()
    start_weights(0)

    lines = half // LANES
    first_line = core * lines

    def column(row):
        return jnp.transpose(jnp.broadcast_to(row, (LANES, LANES)))

    def spread_hot(ref, row0, col):
        for c in range(ref.shape[1] // LANES):
            ids = lax.broadcasted_iota(jnp.int32, (LANES, LANES), 1) + c * LANES
            ref[pl.ds(row0, LANES), c * LANES : (c + 1) * LANES] = jnp.where(
                ids == col, 1.0, 0.0
            ).astype(BF)

    def build_send(i, carry):
        spread_hot(hot_send, pl.multiple_of(i * LANES, LANES), column(send_rows[pl.ds(i, 1), :]))
        return carry

    lax.fori_loop(0, patches, build_send, 0)

    def build_edge(i, carry):
        at = pl.multiple_of(i * LANES, LANES)
        row = recvs[pl.ds(first_line + i, 1), :]
        ids = lax.broadcasted_iota(jnp.int32, (nrows, LANES), 0)
        hot_recv_t[:, pl.ds(at, LANES)] = jnp.where(ids == row, 1.0, 0.0).astype(BF)
        spread_hot(hot_recv, at, column(row))
        spread_hot(hot_slot, at, column(slots[pl.ds(first_line + i, 1), :]))
        return carry

    def table_copy(l, s, d):
        return remote(
            picked.at[pl.ds(pl.multiple_of(d * cap, cap), cap)],
            table.at[
                l,
                pl.ds(pl.multiple_of(s * cap, cap), cap),
                pl.ds(pl.multiple_of(core * half_width, half_width), half_width),
            ],
            sem_ts.at[l, d],
            sem_tr.at[l, s],
            patch=d,
        )

    def table_pass(l, s, c):
        part_of = table.at[
            l,
            pl.ds(pl.multiple_of(s * cap, cap), cap),
            pl.ds(pl.multiple_of(c * half_width, half_width), half_width),
        ]
        return remote(part_of, part_of, sem_fs.at[l, s], sem_fr.at[l, s], feat=mate)

    def bias(row):
        order = sorted(range(feats), key=lambda q: (q % 2) * half_feats + q // 2)
        return jnp.concatenate([all_b[q, row : row + 1, :] for q in order], axis=1)

    def out_local(b):
        rows = pl.ds(pl.multiple_of(b * BLOCK, BLOCK), BLOCK)
        dst = pl.ds(pl.multiple_of(core * half + b * BLOCK, BLOCK), BLOCK)
        return pltpu.make_async_copy(edge.at[rows], edges_out.at[dst], sem_ol.at[b])

    def out_remote(b, c):
        rows = pl.ds(pl.multiple_of(b * BLOCK, BLOCK), BLOCK)
        dst = pl.ds(pl.multiple_of(c * half + b * BLOCK, BLOCK), BLOCK)
        return remote(edge.at[rows], edges_out.at[dst], sem_os.at[b], sem_or.at[b], feat=mate)

    load_nodes.wait()
    for l in range(layers):
        k0 = 6 * l
        advance(k0)
        acquire(k0)
        proj[...] = dot(node[...], w_send[l]).astype(BF)

        def pick(j, carry, l=l):
            d = lax.rem(me + j, patches)
            rows = pl.ds(pl.multiple_of(d * cap, cap), cap)
            picked[rows, :] = dot(hot_send[rows, :], proj[...]).astype(BF)
            table_copy(l, me, d).start()
            return carry

        lax.fori_loop(1, patches, pick, 0)
        mine = pl.ds(pl.multiple_of(me * cap, cap), cap)
        table[
            l, mine, pl.ds(pl.multiple_of(core * half_width, half_width), half_width)
        ] = dot(hot_send[mine, :], proj[...]).astype(BF)
        table_pass(l, me, core).start()
        if l == 0:
            lax.fori_loop(0, lines, build_edge, 0, unroll=2)
            load_edges.wait()
            for j in range(1, feats):
                bias_copy(j, lax.rem(f + feats - j, feats)).wait_recv()
        advance(k0 + 1)
        advance(k0 + 2)
        acquire(k0 + 1)
        acquire(k0 + 2)
        for b in range(nrows // BLOCK):
            rows = slice(b * BLOCK, (b + 1) * BLOCK)
            rproj[rows] = dot(node[rows], w_edge[l, 1]).astype(BF)
        eb_row = bias(l)

        def begin(b, carry, l=l, eb_row=eb_row):
            rows = pl.ds(pl.multiple_of(b * BLOCK, BLOCK), BLOCK)
            pre[rows, :] = (
                dot(edge[rows, :], w_edge[l, 0]) + dot(hot_recv[rows, :], rproj[...]) + eb_row
            )
            return carry

        lax.fori_loop(0, blocks, begin, 0, unroll=2)

        def relay(j, carry, l=l):
            s = lax.rem(me + j, patches)
            table_copy(l, s, me).wait_recv()
            table_pass(l, s, core).start()
            return carry

        lax.fori_loop(1, patches, relay, 0)
        advance(k0 + 3)

        def settle(s, carry, l=l):
            table_pass(l, s, 1 - core).wait_recv()
            return carry

        lax.fori_loop(0, patches, settle, 0)
        acquire(k0 + 3)
        if l + 1 < layers:
            start_weights(l + 1)

        def first(b, l=l):
            rows = pl.ds(pl.multiple_of(b * BLOCK, BLOCK), BLOCK)
            upd[rows, :] = silu(pre[rows, :] + dot(hot_slot[rows, :], table[l])).astype(BF)

        def second(b, l=l):
            rows = pl.ds(pl.multiple_of(b * BLOCK, BLOCK), BLOCK)
            message = norm(dot(upd[rows, :], w_eo[l]), egain[l : l + 1, :])
            upd[rows, :] = message.astype(BF)
            edge[rows, :] = (edge[rows, :].astype(F32) + message).astype(BF)

        def hand_out(b, l=l):
            if l == layers - 1:
                out_local(b).start()
                out_remote(b, core).start()

        def work(b, carry):
            second(b - 1)
            first(b)
            hand_out(b - 1)
            return carry

        first(0)
        lax.fori_loop(1, blocks, work, 0)
        second(blocks - 1)
        hand_out(blocks - 1)
        for b in range(nrows // BLOCK):
            rows = slice(b * BLOCK, (b + 1) * BLOCK)
            part[rows] = dot(hot_recv_t[rows, :], upd[...]).astype(BF)
        swap = remote(part, other.at[l], sem_ps.at[l], sem_pr.at[l], feat=mate)
        swap.start()
        advance(k0 + 4)
        advance(k0 + 5)
        acquire(k0 + 4)
        acquire(k0 + 5)
        npre = pre.at[0:nrows]
        npre[...] = dot(node[...], w_nin[l, 0])
        swap.wait()
        nb_row = bias(layers + l)
        incoming = (part[...].astype(F32) + other[l].astype(F32)).astype(BF)
        hidden = silu(npre[...] + dot(incoming, w_nin[l, 1]) + nb_row).astype(BF)
        change = norm(dot(hidden, w_no[l]), ngain[l : l + 1, :])
        node[...] = (node[...].astype(F32) + change).astype(BF)

        def drain(j, carry, l=l):
            table_copy(l, me, lax.rem(me + j, patches)).wait_send()
            return carry

        lax.fori_loop(1, patches, drain, 0)

    store_nodes = pltpu.make_async_copy(node, nodes_out, sem_in.at[2])
    store_nodes.start()
    for j in range(1, feats):
        bias_copy(j, f).wait_send()
    for k in range(6 * layers):
        for j in range(1, half_feats):
            across(k, j, f).wait_send()
        if k % 6:
            for j in range(half_feats):
                beside(k, j, back(f, j)).wait_send()
    for l in range(layers):

        def done(s, carry, l=l):
            table_pass(l, s, core).wait_send()
            return carry

        lax.fori_loop(0, patches, done, 0)

    def finish(b, carry):
        out_local(b).wait()
        out_remote(b, core).wait_send()
        out_remote(b, 1 - core).wait_recv()
        return carry

    lax.fori_loop(0, blocks, finish, 0)
    store_nodes.wait()


def body(patches, feats, *args):
    (nodes, edges, send_rows, edge_slot, receivers, ein, eb, eo, egain, nin, nb, no, ngain) = args
    layers = ein.shape[0]
    nrows, dim = nodes.shape
    erows = edges.shape[0]
    half = erows // 2
    width = ein.shape[3]
    hid = width * feats
    cap = send_rows.shape[2]
    slots = patches * cap
    blocks = half // BLOCK
    vmem = pltpu.VMEM
    bias_rows = -(-2 * layers // 8) * 8
    dma = pltpu.SemaphoreType.DMA
    any_spec = pl.BlockSpec(memory_space=pl.ANY)
    v_spec = pl.BlockSpec(memory_space=vmem)
    call = pl.pallas_call(
        functools.partial(kernel, patches, feats),
        out_shape=(
            jax.ShapeDtypeStruct((nrows, dim), BF),
            jax.ShapeDtypeStruct((erows, dim), BF),
        ),
        in_specs=[
            any_spec, any_spec, v_spec, v_spec, v_spec, any_spec, v_spec, any_spec, v_spec,
            any_spec, v_spec, any_spec, v_spec,
        ],
        out_specs=(any_spec, any_spec),
        scratch_shapes=[
            vmem((bias_rows, width), F32),
            vmem((feats, bias_rows, width), F32),
            vmem((layers, dim, hid // 2), BF),
            vmem((layers, 2, dim, hid), BF),
            vmem((layers, hid, dim), BF),
            vmem((layers, 2, dim, hid), BF),
            vmem((layers, hid, dim), BF),
            vmem((layers, slots, hid), BF),
            vmem((half, slots), BF),
            vmem((half, nrows), BF),
            vmem((nrows, half), BF),
            vmem((slots, nrows), BF),
            vmem((half, dim), BF),
            vmem((half, hid), F32),
            vmem((half, dim), BF),
            vmem((nrows, dim), BF),
            vmem((nrows, hid // 2), BF),
            vmem((slots, hid // 2), BF),
            vmem((nrows, dim), BF),
            vmem((layers, nrows, dim), BF),
            vmem((nrows, hid), BF),
            dma((3,)),
            dma((6 * layers,)),
            dma((6 * layers, feats // 2)),
            dma((6 * layers, feats // 2)),
            dma((6 * layers, feats // 2)),
            dma((6 * layers, feats // 2)),
            dma((feats,)),
            dma((feats,)),
            dma((layers, patches)),
            dma((layers, patches)),
            dma((layers, patches)),
            dma((layers, patches)),
            dma((layers,)),
            dma((layers,)),
            dma((blocks,)),
            dma((blocks,)),
            dma((blocks,)),
        ],
        compiler_params=pltpu.CompilerParams(
            collective_id=0, has_side_effects=True, vmem_limit_bytes=62 * 2**20
        ),
    )
    return call(
        nodes,
        edges,
        send_rows.reshape(patches, cap),
        edge_slot.reshape(erows // LANES, LANES),
        receivers.reshape(erows // LANES, LANES),
        ein, eb, eo, egain, nin, nb, no, ngain,
    )


def solution(mesh):
    in_specs = (
        P("patch", None),
        P("patch", None),
        P("patch", None, None),
        P("patch"),
        P("patch"),
        P(None, None, None, "feat"),
        P(None, "feat"),
        P(None, "feat", None),
        P(),
        P(None, None, None, "feat"),
        P(None, "feat"),
        P(None, "feat", None),
        P(),
    )
    out_specs = (P("patch", None), P("patch", None))
    inner = functools.partial(body, mesh.shape["patch"], mesh.shape["feat"])
    return jax.shard_map(inner, mesh=mesh, in_specs=in_specs, out_specs=out_specs, check_vma=False)
```
